32 devices in a mesh: pipe: 2 (over x), expert: 16 (over z, y, core).
Axes of the slice: x: 2, y: 2, z: 4, core: 2. Of those that a mesh axis runs over, the one named last changes fastest.
Arguments:
- saved_inputs: bfloat16 [2, 3, 1024, 2048], P('pipe', None, 'expert'), may hold values from -6 to 6
- routes: int32 [2, 3, 1024, 4], P('pipe', None, 'expert'), may hold values from 0 to 15, as said below
- gates: float32 [2, 3, 1024, 4], P('pipe', None, 'expert'), may hold values from 0.1 to 0.6
- w_in: bfloat16 [2, 16, 2048, 768], P('pipe', 'expert'), may hold values from -0.125 to 0.125
- w_out: bfloat16 [2, 16, 768, 2048], P('pipe', 'expert'), may hold values from -0.21875 to 0.21875
- cotangent: bfloat16 [3, 1024, 2048], P(None, 'expert', 'pipe'), may hold values from -6 to 6
Outputs:
- grad_in: bfloat16 [3, 1024, 2048], P(None, 'expert', 'pipe')
- grad_w_in: bfloat16 [2, 16, 2048, 768], P('pipe', 'expert')
- grad_w_out: bfloat16 [2, 16, 768, 2048], P('pipe', 'expert')
The draws below stay inside these ranges and needn't reach their ends.
Inputs may be any that keep to these rules, and one draw needn't show every extreme that they name: `routes`: each token names 4 different experts. Among the 64 tokens of one device's micro-batch (aligned blocks of the token dimension) no expert is named by more than 19 tokens. In every micro-batch of every section some expert is named by exactly 19 tokens in every such block.
All inputs are finite; a program needn't handle non-finite values.
Results may differ from the reference program's by a relative error of at most 0.02.
Values may be sent and summed in bfloat16 or wider, within the bound.
A program may use at most 128 MiB of HBM per device.

```python
import jax
import jax.numpy as jnp
from jax import lax

D = 2048
FF = 768
TOP = 4
MB = 3
TOK_MB = 64
EXPERTS = 16
TOKENS = 1024
CAP = 19
N_PIPE = 2
N_EXPERT = 16


def block_routes(block_key, busiest):
    order_key, weight_key, jitter_key, token_key = jax.random.split(block_key, 4)
    group_size = EXPERTS // TOP
    shuffle_order = jax.random.permutation(order_key, jnp.arange(EXPERTS, dtype=jnp.int32))
    leading = shuffle_order[0]
    shuffle_order = jnp.where(shuffle_order == busiest, leading, shuffle_order)
    shuffle_order = shuffle_order.at[0].set(busiest)
    chosen = shuffle_order[:group_size * TOP].reshape(TOP, group_size)
    weights = jax.random.randint(weight_key, (TOP, group_size), 0, 4)
    jitter = jax.random.randint(jitter_key, (TOP, group_size, CAP), 0, 4096)
    slot_index = jnp.arange(group_size * CAP, dtype=jnp.int32).reshape(group_size, CAP)
    scores = (weights[:, :, None] * 4096 + jitter) * 4096 + slot_index[None, :, :]
    forced = 1073741824 + slot_index[0][None, :]
    scores = scores.at[:, 0, :].set(jnp.broadcast_to(forced, (TOP, CAP)))
    flat_scores = scores.reshape(TOP, group_size * CAP).astype(jnp.int32)
    unused_values, picked = lax.top_k(flat_scores, TOK_MB)
    owner_rank = jnp.sort((picked // CAP).astype(jnp.int32), axis=1)
    column = jnp.take_along_axis(chosen, owner_rank, axis=1)
    token_keys = jax.random.split(token_key, TOP)
    orders = jax.vmap(lambda one_key: jax.random.permutation(one_key, jnp.arange(TOK_MB, dtype=jnp.int32)))(token_keys)
    shuffled = jnp.take_along_axis(column, orders.astype(jnp.int32), axis=1)
    return shuffled.T


def draw_routes(key, part):
    busy_key, blocks_key = jax.random.split(jax.random.fold_in(key, 7))
    busiest = jax.random.randint(busy_key, (N_PIPE * MB,), 0, EXPERTS).astype(jnp.int32)
    block_keys = jax.random.split(blocks_key, N_PIPE * MB * N_EXPERT)
    busiest_rep = jnp.repeat(busiest, N_EXPERT)
    blocks = jax.vmap(block_routes)(block_keys, busiest_rep)
    return blocks.reshape(N_PIPE, MB, TOKENS, TOP).astype(jnp.int32)


def block_scale(stream_key, extent, shards, smallest, largest):
    level = 1.0
    for position, blocks in shards:
        steps = jax.random.uniform(jax.random.fold_in(jax.random.fold_in(stream_key, 6), position), (blocks,), jnp.float32, smallest / len(shards), largest / len(shards))
        level = level * jnp.repeat(jnp.exp(steps), extent[position] // blocks).reshape((-1,) + (1,) * (len(extent) - 1 - position))
    return level


def centred(rng, extent, deviation, bound, cuts=(), kind=jnp.bfloat16):
    result = jax.random.normal(rng, extent, jnp.float32) * deviation
    if len(cuts) > 0:
        result = block_scale(rng, extent, cuts, -0.22, 0.18) * result
    return jnp.clip(result, min=-bound, max=bound).astype(kind)


def setup_inputs(seed: int = 0) -> dict:
    splits = jax.random.split(jax.random.key(seed), 7)
    return {
        "saved_inputs": centred(splits[0], (N_PIPE, MB, TOKENS, D), 1.0, 6.0, ((0, 2), (2, 16))),
        "routes": draw_routes(jax.random.fold_in(splits[6], 71), 0),
        "gates": jnp.clip(0.1 + 0.5 * jax.random.uniform(splits[2], (N_PIPE, MB, TOKENS, TOP), jnp.float32) ** block_scale(splits[2], (N_PIPE, MB, TOKENS, TOP), ((0, 2), (2, 16)), -0.2, 0.2), 0.1, 0.6),
        "w_in": centred(splits[3], (N_PIPE, EXPERTS, D, FF), D ** -0.5, 0.125, ((0, 2), (1, 16))),
        "w_out": centred(splits[4], (N_PIPE, EXPERTS, FF, D), FF ** -0.5, 0.21875, ((0, 2), (1, 16))),
        "cotangent": centred(splits[5], (MB, TOKENS, D), 1.0, 6.0, ((1, 16), (2, 2))),
    }


def silu_slope(preactivation):
    logistic = jax.nn.sigmoid(preactivation)
    return logistic * (1.0 + preactivation * (1.0 - logistic))


def slot_numbers(routes_micro):
    per_block = routes_micro.reshape(N_EXPERT, TOK_MB * TOP)
    expert_ids = jnp.arange(EXPERTS, dtype=jnp.int32)
    one_hot = (per_block[:, :, None] == expert_ids[None, None, :]).astype(jnp.int32)
    ranks = jnp.sum((jnp.cumsum(one_hot, axis=1) - 1) * one_hot, axis=2)
    block_ids = jnp.arange(N_EXPERT, dtype=jnp.int32)[:, None]
    slots = per_block * (N_EXPERT * CAP) + block_ids * CAP + ranks
    return slots.reshape(-1).astype(jnp.int32)


def expert_rows(operands):
    input_rows, grad_rows, first_weight, second_weight = operands
    preactivation = jnp.dot(input_rows, first_weight, preferred_element_type=jnp.float32)
    hidden_grad = jnp.dot(grad_rows, second_weight.T, preferred_element_type=jnp.float32)
    pre_grad = (hidden_grad * silu_slope(preactivation)).astype(jnp.bfloat16)
    hidden = jax.nn.silu(preactivation).astype(jnp.bfloat16)
    row_grads = jnp.dot(pre_grad, first_weight.T, preferred_element_type=jnp.float32).astype(jnp.bfloat16)
    first_grad = jnp.dot(input_rows.T, pre_grad, preferred_element_type=jnp.float32).astype(jnp.bfloat16)
    second_grad = jnp.dot(hidden.T, grad_rows, preferred_element_type=jnp.float32).astype(jnp.bfloat16)
    return row_grads, first_grad, second_grad


def section_pass(inputs_section, routes_section, gates_section, grad_section, first_weights, second_weights):
    total_slots = EXPERTS * N_EXPERT * CAP
    slot_list, input_parts, grad_parts = [], [], []
    for micro_no in range(MB):
        slots = slot_numbers(routes_section[micro_no])
        input_rep = jnp.repeat(inputs_section[micro_no], TOP, axis=0)
        gate_scaled_rows = (gates_section[micro_no][:, :, None] * grad_section[micro_no].astype(jnp.float32)[:, None, :]).astype(jnp.bfloat16)
        gate_scaled_rows = gate_scaled_rows.reshape(TOKENS * TOP, D)
        input_slots = jnp.zeros((total_slots, D), input_rep.dtype).at[slots].set(input_rep)
        gradient_slot_buffer = jnp.zeros((total_slots, D), gate_scaled_rows.dtype).at[slots].set(gate_scaled_rows)
        slot_list.append(slots)
        input_parts.append(input_slots.reshape(EXPERTS, N_EXPERT * CAP, D))
        grad_parts.append(gradient_slot_buffer.reshape(EXPERTS, N_EXPERT * CAP, D))
    input_all = jnp.concatenate(input_parts, axis=1)
    grad_all = jnp.concatenate(grad_parts, axis=1)
    row_grads, first_grad, second_grad = lax.map(expert_rows, (input_all, grad_all, first_weights, second_weights))
    span = N_EXPERT * CAP
    results = []
    for micro_no in range(MB):
        part = row_grads[:, micro_no * span:(micro_no + 1) * span, :].reshape(total_slots, D)
        returned = part[slot_list[micro_no]].astype(jnp.float32).reshape(TOKENS, TOP, D)
        grad_inputs = (grad_section[micro_no].astype(jnp.float32) + jnp.sum(returned, axis=1)).astype(jnp.bfloat16)
        results.append(grad_inputs)
    return jnp.stack(results), first_grad, second_grad


def reference(saved_inputs, routes, gates, w_in, w_out, cotangent):
    section_grad = cotangent
    firsts, seconds = [], []
    for section_no in range(N_PIPE - 1, -1, -1):
        section_grad, first_grad, second_grad = section_pass(saved_inputs[section_no], routes[section_no], gates[section_no], section_grad, w_in[section_no], w_out[section_no])
        firsts.insert(0, first_grad)
        seconds.insert(0, second_grad)
    return section_grad, jnp.stack(firsts), jnp.stack(seconds)
```

```python
import jax
import jax.numpy as jnp
from jax import lax
from jax.sharding import PartitionSpec as P


def after(value, earlier):
    nothing = jnp.minimum(jnp.abs(earlier[0, 0].astype(jnp.float32)), 0.0)
    return value + nothing.astype(value.dtype)


def placement(routes_micro, gates_micro, expert_count, capacity):
    tokens, tops = routes_micro.shape
    flat = routes_micro.reshape(-1)
    count = tokens * tops
    one_hot = (flat[:, None] == jnp.arange(expert_count, dtype=jnp.int32)[None, :]).astype(jnp.bfloat16)
    order = jnp.arange(count, dtype=jnp.int32)
    before = (order[:, None] > order[None, :]).astype(jnp.bfloat16)
    earlier = jnp.dot(before, one_hot, preferred_element_type=jnp.float32)
    ranks = jnp.sum(earlier * one_hot.astype(jnp.float32), axis=1).astype(jnp.int32)
    slots = (flat * capacity + ranks).reshape(tokens, tops)
    slot_ids = jnp.arange(expert_count * capacity, dtype=jnp.int32)
    table = jnp.zeros((expert_count * capacity, tokens), jnp.float32)
    slot_gates = jnp.zeros((expert_count * capacity,), jnp.float32)
    for top in range(tops):
        hit = slot_ids[:, None] == slots[:, top][None, :]
        table = table + hit.astype(jnp.float32)
        slot_gates = slot_gates + jnp.sum(jnp.where(hit, gates_micro[:, top][None, :], 0.0), axis=1)
    return table.astype(jnp.bfloat16), slot_gates


def exchange(rows):
    return lax.all_to_all(rows, "expert", split_axis=0, concat_axis=0, tiled=True)


def pick(index, values):
    result = values[-1]
    for number in range(len(values) - 2, -1, -1):
        result = jnp.where(index <= number, values[number], result)
    return result


def on_device(saved_inputs, routes, gates, w_in, w_out, cotangent):
    sections = lax.axis_size("pipe")
    section = lax.axis_index("pipe")
    micros = saved_inputs.shape[1]
    tokens = saved_inputs.shape[2]
    experts = w_in.shape[1] * lax.axis_size("expert")
    capacity = max(2, tokens * routes.shape[3] * 6 // (5 * experts))
    ticks = sections + micros - 1
    first_tick = sections - 1 - section
    last = section == sections - 1
    weight_in, weight_out = w_in[0, 0], w_out[0, 0]
    width = cotangent.shape[2]

    places = [placement(routes[0, m], gates[0, m], experts, capacity) for m in range(micros)]
    tables = [place[0] for place in places]
    slot_gates = [place[1] for place in places]

    def upstream(m):
        own = cotangent[m]
        parts = [
            lax.ppermute(own, "pipe", [(sender, sections - 1)]) for sender in range(sections - 1)
        ]
        return jnp.concatenate(parts + [own], axis=1)

    def send_inputs(m, earlier):
        table = tables[m] if earlier is None else after(tables[m], earlier)
        return exchange(
            jnp.dot(table, saved_inputs[0, m], preferred_element_type=jnp.float32).astype(jnp.bfloat16)
        )

    input_recv, slopes, hiddens = [], [], []

    def take_inputs(received):
        pre = jnp.dot(received, weight_in, preferred_element_type=jnp.float32)
        logistic = jax.nn.sigmoid(pre)
        input_recv.append(received)
        slopes.append(logistic * (1.0 + pre * (1.0 - logistic)))
        hiddens.append((pre * logistic).astype(jnp.bfloat16))

    take_inputs(send_inputs(0, None))
    incoming = None
    grads, pre_grads, outs = [], [], []
    for tick in range(ticks):
        micro = tick - first_tick
        if tick < micros:
            grad_now = upstream(tick)
            if incoming is not None:
                grad_now = jnp.where(last, grad_now, incoming)
        else:
            grad_now = incoming
        table = pick(micro, tables)
        slot_gate = pick(micro, slot_gates)
        if tick == 0:
            table = after(table, input_recv[0])
        placed = jnp.dot(table, grad_now, preferred_element_type=jnp.float32)
        grad_recv = exchange((placed * slot_gate[:, None]).astype(jnp.bfloat16))
        if tick == 0 and micros > 1:
            take_inputs(send_inputs(1, grad_recv))
        hidden_grad = lax.dot_general(
            grad_recv, weight_out, (((1,), (1,)), ((), ())), preferred_element_type=jnp.float32
        )
        known = [slopes[m] for m in range(min(tick + 1, micros))]
        pre_grad = (hidden_grad * pick(micro, known)).astype(jnp.bfloat16)
        row_grads = lax.dot_general(
            pre_grad, weight_in, (((1,), (1,)), ((), ())), preferred_element_type=jnp.float32
        ).astype(jnp.bfloat16)
        returned = exchange(row_grads)
        if tick + 2 < micros:
            take_inputs(send_inputs(tick + 2, returned))
        summed = lax.dot_general(
            table, returned, (((0,), (0,)), ((), ())), preferred_element_type=jnp.float32
        )
        grad_out = (grad_now.astype(jnp.float32) + summed).astype(jnp.bfloat16)
        grads.append(grad_recv)
        pre_grads.append(pre_grad)
        outs.append(grad_out)
        if tick + 1 < ticks:
            incoming = lax.ppermute(
                grad_out, "pipe", [(source, source - 1) for source in range(1, sections)]
            )

    def across(left, right):
        return lax.dot_general(
            left, right, (((0,), (0,)), ((), ())), preferred_element_type=jnp.float32
        )

    grad_in = []
    for m in range(micros):
        rows = outs[sections - 1 + m]
        result = jnp.where(section == 0, rows[:, :width], 0)
        for target in range(1, sections):
            part = rows[:, target * width : (target + 1) * width]
            result = result + lax.ppermute(part, "pipe", [(0, target)])
        grad_in.append(result)

    first, second = 0.0, 0.0
    for m in range(micros):
        mine = pick(first_tick, pre_grads[m : m + sections])
        first = first + across(input_recv[m], mine)
    for tick in range(ticks):
        micro = tick - first_tick
        valid = (micro >= 0) & (micro < micros)
        hidden = jnp.where(valid, pick(micro, hiddens), 0)
        second = second + across(hidden, grads[tick])
    return (
        jnp.stack(grad_in),
        first.astype(jnp.bfloat16)[None, None],
        second.astype(jnp.bfloat16)[None, None],
    )


def solution(mesh):
    return jax.shard_map(
        on_device,
        mesh=mesh,
        in_specs=(
            P("pipe", None, "expert", None),
            P("pipe", None, "expert", None),
            P("pipe", None, "expert", None),
            P("pipe", "expert", None, None),
            P("pipe", "expert", None, None),
            P(None, "expert", "pipe"),
        ),
        out_specs=(
            P(None, "expert", "pipe"),
            P("pipe", "expert", None, None),
            P("pipe", "expert", None, None),
        ),
        check_vma=False,
    )
```

```python
import functools
import math

import jax
import jax.numpy as jnp
from jax import lax
from jax.experimental import pallas as pl
from jax.experimental.pallas import tpu as pltpu
from jax.sharding import PartitionSpec as P


def after(value, earlier):
    nothing = jnp.minimum(jnp.abs(earlier[0, 0].astype(jnp.float32)), 0.0)
    return value + nothing.astype(value.dtype)


def placement(routes_micro, expert_count, capacity):
    tokens, tops = routes_micro.shape
    flat = routes_micro.reshape(-1)
    count = tokens * tops
    one_hot = (flat[:, None] == jnp.arange(expert_count, dtype=jnp.int32)[None, :]).astype(jnp.bfloat16)
    order = jnp.arange(count, dtype=jnp.int32)
    before = (order[:, None] > order[None, :]).astype(jnp.bfloat16)
    earlier = jnp.dot(before, one_hot, preferred_element_type=jnp.float32)
    ranks = jnp.sum(earlier * one_hot.astype(jnp.float32), axis=1).astype(jnp.int32)
    slots = (flat * capacity + ranks).reshape(tokens, tops)
    slot_ids = jnp.arange(expert_count * capacity, dtype=jnp.int32)
    table = jnp.zeros((expert_count * capacity, tokens), jnp.float32)
    for top in range(tops):
        hit = slot_ids[:, None] == slots[:, top][None, :]
        table = table + hit.astype(jnp.float32)
    return table.astype(jnp.bfloat16)


def exchange(rows):
    return lax.all_to_all(rows, "expert", split_axis=0, concat_axis=0, tiled=True)


def gather_kernel(depth, height, arrays, *refs):
    block_refs, out_refs = refs[:arrays], refs[arrays : 2 * arrays]
    send_sems, recv_sems, own_sems = refs[2 * arrays :]
    me = lax.axis_index("expert")
    core = lax.rem(me, 2)
    y = lax.rem(me // 2, height)
    z = me // (2 * height)

    def place(z_at, y_at, core_at):
        return (z_at * height + y_at) * 2 + core_at

    up, down, right, left, across = range(5)
    targets = {
        up: (place(z + 1, y, core), z < depth - 1),
        down: (place(z - 1, y, core), z > 0),
        right: (place(z, y + 1, core), y < height - 1),
        left: (place(z, y - 1, core), y > 0),
        across: (place(z, y, 1 - core), None),
    }

    def guarded(condition, action):
        if condition is None:
            action()
        else:
            pl.when(condition)(action)

    barrier = pltpu.get_barrier_semaphore()
    for target, exists in targets.values():
        guarded(
            exists,
            functools.partial(
                pl.semaphore_signal,
                barrier,
                inc=1,
                device_id={"expert": target},
                device_id_type=pl.DeviceIdType.MESH,
            ),
        )
    owns = [
        pltpu.make_async_copy(block_refs[k], out_refs[k].at[me], own_sems.at[k]) for k in range(arrays)
    ]
    for own in owns:
        own.start()
    neighbours = jnp.int32(1)
    for _, exists in targets.values():
        if exists is not None:
            neighbours = neighbours + jnp.where(exists, 1, 0)
    pl.semaphore_wait(barrier, neighbours)

    sends = []

    def copy(k, way, owner, mine):
        return pltpu.make_async_remote_copy(
            src_ref=block_refs[k] if mine else out_refs[k].at[owner],
            dst_ref=out_refs[k].at[owner],
            send_sem=send_sems.at[k, way, owner],
            recv_sem=recv_sems.at[k, owner],
            device_id={"expert": targets[way][0]},
            device_id_type=pl.DeviceIdType.MESH,
        )

    def arrived(owner):
        for k in range(arrays):
            copy(k, across, owner, False).wait_recv()

    def forward(owner, ways, present, mine=False):
        for way in ways:
            exists = targets[way][1]
            if present is not None:
                exists = present if exists is None else present & exists
            sends.append((way, owner, exists, mine))

            def begin(way=way):
                for k in range(arrays):
                    copy(k, way, owner, mine).start()

            guarded(exists, begin)

    forward(me, (up, down, right, left, across), None, True)
    for step in range(1, depth + height - 1):
        for y_gap in range(min(step, height - 1) + 1):
            z_gap = step - y_gap
            if z_gap > depth - 1:
                continue
            for z_sign in (1, -1) if z_gap else (1,):
                for y_sign in (1, -1) if y_gap else (1,):
                    z_from, y_from = z - z_sign * z_gap, y - y_sign * y_gap
                    present = (z_from >= 0) & (z_from < depth) & (y_from >= 0) & (y_from < height)
                    owner = place(z_from, y_from, core)
                    pl.when(present)(functools.partial(arrived, owner))
                    if y_gap:
                        ways = (right if y_sign > 0 else left, across)
                    else:
                        ways = (up if z_sign > 0 else down, right, left, across)
                    forward(owner, ways, present)
    for column in range(depth * height):
        arrived(column * 2 + 1 - core)
    for way, owner, exists, mine in sends:

        def finish():
            for k in range(arrays):
                copy(k, way, owner, mine).wait_send()

        guarded(exists, finish)
    for own in owns:
        own.wait()


def gather(*blocks):
    owners = lax.axis_size("expert")
    height = math.isqrt(owners // 4)
    depth = owners // (2 * height)
    arrays = len(blocks)
    size = sum(block.size * block.dtype.itemsize for block in blocks)
    return pl.pallas_call(
        functools.partial(gather_kernel, depth, height, arrays),
        out_shape=[jax.ShapeDtypeStruct((owners, *block.shape), block.dtype) for block in blocks],
        in_specs=[pl.BlockSpec(memory_space=pltpu.VMEM)] * arrays,
        out_specs=[pl.BlockSpec(memory_space=pltpu.VMEM)] * arrays,
        scratch_shapes=[
            pltpu.SemaphoreType.DMA((arrays, 5, owners)),
            pltpu.SemaphoreType.DMA((arrays, owners)),
            pltpu.SemaphoreType.DMA((arrays,)),
        ],
        compiler_params=pltpu.CompilerParams(
            collective_id=arrays,
            has_side_effects=True,
            vmem_limit_bytes=(owners + 2) * size + 2 * 1024 * 1024,
        ),
        cost_estimate=pl.CostEstimate(flops=0, bytes_accessed=20 * owners * size, transcendentals=0),
    )(*blocks)


def rows_of(gathered):
    return gathered.reshape(gathered.shape[0] * gathered.shape[1], gathered.shape[2])


def arrivals(routes_all, gates_all, me, capacity):
    owners, _, tokens = routes_all.shape
    hit = routes_all == me.astype(jnp.float32)
    named = jnp.sum(hit.astype(jnp.float32), axis=1)
    gate = jnp.sum(jnp.where(hit, gates_all, 0.0), axis=1)
    order = jnp.arange(tokens, dtype=jnp.int32)
    before = (order[:, None] < order[None, :]).astype(jnp.bfloat16)
    ranks = jnp.dot(named.astype(jnp.bfloat16), before, preferred_element_type=jnp.float32)
    starts = jnp.arange(owners, dtype=jnp.int32)[:, None] * capacity
    slots = jnp.where(named > 0, starts + ranks.astype(jnp.int32), -1).reshape(1, -1)
    slot_ids = jnp.arange(owners * capacity, dtype=jnp.int32)[:, None]
    chosen = (slot_ids == slots).astype(jnp.bfloat16)
    high = lax.reduce_precision(gate, 8, 7)
    middle = lax.reduce_precision(gate - high, 8, 7)
    pieces = jnp.stack([high, middle, gate - high - middle]).reshape(3, -1).astype(jnp.bfloat16)
    split = lax.dot_general(
        chosen, pieces, (((1,), (1,)), ((), ())), preferred_element_type=jnp.float32
    )
    return chosen, split[:, 0] + split[:, 1] + split[:, 2]


def pick(index, values):
    result = values[-1]
    for number in range(len(values) - 2, -1, -1):
        result = jnp.where(index <= number, values[number], result)
    return result


def on_device(saved_inputs, routes, gates, w_in, w_out, cotangent):
    sections = lax.axis_size("pipe")
    section = lax.axis_index("pipe")
    micros = saved_inputs.shape[1]
    tokens = saved_inputs.shape[2]
    experts = w_in.shape[1] * lax.axis_size("expert")
    capacity = max(2, tokens * routes.shape[3] * 6 // (5 * experts))
    ticks = sections + micros - 1
    first_tick = sections - 1 - section
    last = section == sections - 1
    weight_in, weight_out = w_in[0, 0], w_out[0, 0]
    width = cotangent.shape[2]

    me = lax.axis_index("expert")
    tables = [placement(routes[0, m], experts, capacity) for m in range(micros)]
    tops = routes.shape[3]
    facts = jnp.concatenate([routes[0].astype(jnp.float32), gates[0]], axis=2).transpose(0, 2, 1)
    facts = jnp.pad(
        facts.reshape(micros * 2 * tops, tokens), ((0, 0), (0, -tokens % 128))
    )

    def upstream(m):
        own = cotangent[m]
        parts = [
            lax.ppermute(own, "pipe", [(sender, sections - 1)]) for sender in range(sections - 1)
        ]
        return jnp.concatenate(parts + [own], axis=1)

    first_block, facts_all = gather(saved_inputs[0, 0], facts)
    owners = facts_all.shape[0]
    facts_all = facts_all[:, :, :tokens].reshape(owners, micros, 2 * tops, tokens)
    taken = [
        arrivals(facts_all[:, m, :tops], facts_all[:, m, tops:], me, capacity) for m in range(micros)
    ]
    take_tables = [part[0] for part in taken]
    slot_gates = [part[1] for part in taken]

    def take_rows(m, gathered):
        return jnp.dot(take_tables[m], rows_of(gathered), preferred_element_type=jnp.float32).astype(
            jnp.bfloat16
        )

    def send_inputs(m, earlier):
        return take_rows(m, gather(after(saved_inputs[0, m], earlier))[0])

    input_recv, slopes, hiddens = [], [], []

    def take_inputs(received):
        pre = jnp.dot(received, weight_in, preferred_element_type=jnp.float32)
        logistic = jax.nn.sigmoid(pre)
        input_recv.append(received)
        slopes.append(logistic * (1.0 + pre * (1.0 - logistic)))
        hiddens.append((pre * logistic).astype(jnp.bfloat16))

    take_inputs(take_rows(0, first_block))
    incoming = None
    grads, pre_grads, outs = [], [], []
    for tick in range(ticks):
        micro = tick - first_tick
        if tick < micros:
            grad_now = upstream(tick)
            if incoming is not None:
                grad_now = jnp.where(last, grad_now, incoming)
        else:
            grad_now = incoming
        table = pick(micro, tables)
        slot_gate = pick(micro, slot_gates)
        placed = jnp.dot(
            pick(micro, take_tables),
            rows_of(gather(after(grad_now, first_block[0]) if tick == 0 else grad_now)[0]),
            preferred_element_type=jnp.float32,
        )
        grad_recv = (placed * slot_gate[:, None]).astype(jnp.bfloat16)
        if tick == 0 and micros > 1:
            take_inputs(send_inputs(1, grad_recv))
        hidden_grad = lax.dot_general(
            grad_recv, weight_out, (((1,), (1,)), ((), ())), preferred_element_type=jnp.float32
        )
        known = [slopes[m] for m in range(min(tick + 1, micros))]
        pre_grad = (hidden_grad * pick(micro, known)).astype(jnp.bfloat16)
        row_grads = lax.dot_general(
            pre_grad, weight_in, (((1,), (1,)), ((), ())), preferred_element_type=jnp.float32
        ).astype(jnp.bfloat16)
        returned = exchange(row_grads)
        if tick + 2 < micros:
            take_inputs(send_inputs(tick + 2, returned))
        summed = lax.dot_general(
            table, returned, (((0,), (0,)), ((), ())), preferred_element_type=jnp.float32
        )
        grad_out = (grad_now.astype(jnp.float32) + summed).astype(jnp.bfloat16)
        grads.append(grad_recv)
        pre_grads.append(pre_grad)
        outs.append(grad_out)
        if tick + 1 < ticks:
            incoming = lax.ppermute(
                grad_out, "pipe", [(source, source - 1) for source in range(1, sections)]
            )

    def across(left, right):
        return lax.dot_general(
            left, right, (((0,), (0,)), ((), ())), preferred_element_type=jnp.float32
        )

    grad_in = []
    for m in range(micros):
        rows = outs[sections - 1 + m]
        result = jnp.where(section == 0, rows[:, :width], 0)
        for target in range(1, sections):
            part = rows[:, target * width : (target + 1) * width]
            result = result + lax.ppermute(part, "pipe", [(0, target)])
        grad_in.append(result)

    first, second = 0.0, 0.0
    for m in range(micros):
        mine = pick(first_tick, pre_grads[m : m + sections])
        first = first + across(input_recv[m], mine)
    for tick in range(ticks):
        micro = tick - first_tick
        valid = (micro >= 0) & (micro < micros)
        hidden = jnp.where(valid, pick(micro, hiddens), 0)
        second = second + across(hidden, grads[tick])
    return (
        jnp.stack(grad_in),
        first.astype(jnp.bfloat16)[None, None],
        second.astype(jnp.bfloat16)[None, None],
    )


def solution(mesh):
    return jax.shard_map(
        on_device,
        mesh=mesh,
        in_specs=(
            P("pipe", None, "expert", None),
            P("pipe", None, "expert", None),
            P("pipe", None, "expert", None),
            P("pipe", "expert", None, None),
            P("pipe", "expert", None, None),
            P(None, "expert", "pipe"),
        ),
        out_specs=(
            P(None, "expert", "pipe"),
            P("pipe", "expert", None, None),
            P("pipe", "expert", None, None),
        ),
        check_vma=False,
    )
```
